512 devices in a mesh: dp: 512 (over x, y, z, core).
Axes of the slice: x: 4, y: 8, z: 8, core: 2. Of those that a mesh axis runs over, the one named last changes fastest.
Arguments:
- pooled: bfloat16 [65536, 768], P('dp'), may hold values from -0.19921875 to 0.19921875
- other_part: bfloat16 [65536, 1152], P('dp'), may hold values from -0.19921875 to 0.19921875
- head_weight: bfloat16 [512, 1728], P('dp'), may hold values from -0.21875 to 0.21875
- text: bfloat16 [65536, 1152], P('dp'), may hold values from -0.19921875 to 0.19921875
- logit_scale: float32 [1], replicated, may hold values from 0.5 to 1.5
- logit_bias: float32 [1], replicated, may hold values from -3 to -1
Outputs:
- pooled_grad: bfloat16 [65536, 768], P('dp')
- text_grad: float32 [65536, 1152], P('dp')
- weight_grad: float32 [512, 1728], P('dp')
The draws below stay inside these ranges and needn't reach their ends.
All inputs are finite; a program needn't handle non-finite values.
Results may differ from the reference program's by a relative error of at most 0.0065.
Values may be sent and summed in bfloat16 or wider, within the bound.
A program may use at most 64 MiB of HBM per device.

```python
import jax
import jax.numpy as jnp
from jax import lax

D = 1152
KW = 768
TOK_DEV = 128
WINDOW = 6
TOKENS = 65536
GROUP = 1728
N_DP = 512


def level_of(key, extent, shards, least, largest):
    factor_of = 1.0
    for dim, blocks in shards:
        heights = jax.random.uniform(jax.random.fold_in(jax.random.fold_in(key, 6), dim), (blocks,), jnp.float32, least / len(shards), largest / len(shards))
        factor_of = factor_of * jnp.repeat(jnp.exp(heights), extent[dim] // blocks).reshape((-1,) + (1,) * (len(extent) - 1 - dim))
    return factor_of


def centred(stream_key, shape, scale, bound, pieces=(), kind=jnp.bfloat16):
    level = level_of(stream_key, shape, pieces, -0.22, 0.18) if pieces else 1.0
    array = jax.random.normal(stream_key, shape, jnp.float32) * scale * level
    return jnp.minimum(jnp.maximum(array, -bound), bound).astype(kind)


def setup_inputs(seed: int = 0) -> dict:
    keys = jax.random.split(jax.random.key(seed), 7)
    return {
        "pooled": centred(keys[0], (TOKENS, KW), 0.03, 0.19921875, ((0, 512),)),
        "other_part": centred(keys[1], (TOKENS, D), 0.03, 0.19921875, ((0, 512),)),
        "head_weight": centred(keys[2], (N_DP, GROUP), KW ** -0.5, 0.21875, ((0, 512),)),
        "text": centred(keys[3], (TOKENS, D), 0.03, 0.19921875, ((0, 512),)),
        "logit_scale": jnp.clip(jax.random.uniform(keys[4], (1,), jnp.float32, 0.5, 1.5), 0.5, 1.5),
        "logit_bias": jnp.clip(jax.random.uniform(keys[5], (1,), jnp.float32, -3.0, -1.0), -3.0, -1.0),
    }


def reference(pooled, other_part, head_weight, text, logit_scale, logit_bias):
    weight = head_weight.reshape(KW, D)
    image = jnp.dot(pooled, weight, preferred_element_type=jnp.float32) + other_part.astype(jnp.float32)
    image_norm = jnp.sqrt(lax.optimization_barrier(jnp.sum(image * image, axis=1, keepdims=True)) + 1e-06)
    image_unit = image / image_norm
    image_emb = image_unit.astype(jnp.bfloat16)
    text_wide = text.astype(jnp.float32)
    text_norm = jnp.sqrt(lax.optimization_barrier(jnp.sum(text_wide * text_wide, axis=1, keepdims=True)) + 1e-06)
    text_unit = text_wide / text_norm
    text_emb = text_unit.astype(jnp.bfloat16)
    temper = jnp.exp(logit_scale[0])
    bias = logit_bias[0]
    img_blocks = image_emb.reshape(N_DP, TOK_DEV, D).astype(jnp.float32)
    txt_blocks = text_emb.reshape(N_DP, TOK_DEV, D)
    eye_mat = jnp.eye(TOK_DEV, dtype=jnp.float32)
    half = WINDOW // 2
    image_emb_grad = jnp.zeros((N_DP, TOK_DEV, D), jnp.float32)
    text_emb_grad = jnp.zeros((N_DP, TOK_DEV, D), jnp.float32)
    for offset in range(-half, half):
        partner = jnp.roll(txt_blocks, offset, axis=0).astype(jnp.float32)
        logits = temper * jnp.einsum('bik,bjk->bij', img_blocks, partner) + bias
        if offset == 0:
            label = 2.0 * eye_mat - 1.0
        else:
            label = -jnp.ones_like(eye_mat)
        coef = (temper * (-label * jax.nn.sigmoid(-label * logits))).astype(jnp.bfloat16).astype(jnp.float32)
        image_emb_grad = image_emb_grad + jnp.einsum('bij,bjk->bik', coef, partner)
        term = jnp.einsum('bij,bik->bjk', coef, img_blocks)
        text_emb_grad = text_emb_grad + jnp.roll(term, -offset, axis=0)
    image_emb_grad = image_emb_grad.reshape(TOKENS, D)
    text_emb_grad = text_emb_grad.reshape(TOKENS, D)
    image_grad = ((image_emb_grad - image_unit * lax.optimization_barrier(jnp.sum(image_unit * image_emb_grad, axis=1, keepdims=True))) / image_norm).astype(jnp.bfloat16)
    pooled_grad = lax.dot_general(image_grad, weight, (((1,), (1,)), ((), ())), preferred_element_type=jnp.float32).astype(jnp.bfloat16)
    weight_grad = lax.dot_general(pooled, image_grad, (((0,), (0,)), ((), ())), preferred_element_type=jnp.float32).reshape(N_DP, GROUP)
    text_grad = (text_emb_grad - text_unit * lax.optimization_barrier(jnp.sum(text_unit * text_emb_grad, axis=1, keepdims=True))) / text_norm
    return (pooled_grad, text_grad, weight_grad)
```

```python
import functools

import jax
import jax.numpy as jnp
from jax import lax
from jax.experimental import pallas as pl
from jax.experimental.pallas import tpu as pltpu
from jax.sharding import PartitionSpec as P

D = 1152
GROUP = 1728
LANES = 128
TILES = 14
HALF = 896
WINDOW = 6
X, Y, Z = 4, 8, 8
EPS = 1e-06
F32 = jnp.float32
BF16 = jnp.bfloat16
MESH = pl.DeviceIdType.MESH


def dot(a, b):
    return jnp.dot(a, b, preferred_element_type=F32)


def dot_t(a, b):
    return lax.dot_general(a, b, (((1,), (1,)), ((), ())), preferred_element_type=F32)


def ring_order(n):
    return sorted(range(1, n), key=lambda d: (min(d, n - d), d))


def kernel(
    dims,
    pooled_ref, other_ref, shard_ref, text_ref, scale_ref, bias_ref,
    pooled_grad_ref, text_grad_ref, weight_grad_ref,
    fold, column, wbuf, bpart, tbuf, ibuf, pool2, grad2, qmat, pat, pbt,
    gsend, gown, grecv, ysend, yown, yrecv, zsend, zrecv,
    col_s, col_r, wy_s, wy_r, wx_s, wx_r, wsib_s, wsib_r,
    text_s, text_r, img_s, img_r, pair_s, pair_r,
    gx_s, gx_r, gy_s, gy_r, gz_s, gz_r,
):
    nx, ny, nz = dims
    count = nx * ny * nz * 2
    rows = 2 * nz
    span = ny * rows
    tok = pooled_ref.shape[0]
    kw = pooled_ref.shape[1]
    chips = count // 2

    me = lax.axis_index("dp")
    c = me % 2
    z = (me // 2) % nz
    y = (me // (2 * nz)) % ny
    x = me // (2 * nz * ny)
    sib = me + 1 - 2 * c

    def device(xx, yy, zz, cc):
        return ((xx * ny + yy) * nz + zz) * 2 + cc

    def ring(step):
        return (me + step + count) % count

    def send(src, dst, ssem, rsem, to):
        pltpu.make_async_remote_copy(
            src_ref=src, dst_ref=dst, send_sem=ssem, recv_sem=rsem, device_id=(to,), device_id_type=MESH
        ).start()

    def wait(ref, sem):
        pltpu.make_async_copy(ref, ref, sem).wait()

    ydist = ring_order(ny)
    xdist = ring_order(nx)

    barrier = pltpu.get_barrier_semaphore()

    def hello(to):
        pl.semaphore_signal(barrier, inc=1, device_id=(to,), device_id_type=MESH)

    def hello_column(i, carry):
        hello(device(x, y, (z + i // 2) % nz, (c + i) % 2))
        return carry

    lax.fori_loop(1, 2 * nz, hello_column, 0)
    for d in ydist:
        hello(device(x, (y + d) % ny, z, c))
    for d in xdist:
        hello(device((x + d) % nx, y, z, c))
    for d in (-3, -2, -1, 1, 2, 3):
        hello(ring(d))

    piece = shard_ref[...].astype(F32)
    fold[...] = jnp.zeros_like(fold)
    for r in range(TILES - 1):
        fold[r : r + 1, :] = piece[:, r * LANES : (r + 1) * LANES]
    fold[TILES - 1 : TILES, : LANES // 2] = piece[:, (TILES - 1) * LANES :]
    slot = c * nz + z
    column[slot] = fold[...].astype(BF16)

    text = text_ref[...].astype(F32)
    text_inv = 1.0 / jnp.sqrt(jnp.sum(text * text, axis=1, keepdims=True) + EPS)
    tbuf[2] = (text * text_inv).astype(BF16)
    pool2[c] = pooled_ref[...]

    pl.semaphore_wait(barrier, 2 * nz - 1 + len(ydist) + len(xdist) + 6)

    def send_column(i, carry):
        to = device(x, y, (z + i // 2) % nz, (c + i) % 2)
        send(column.at[slot], column.at[slot], col_s.at[i], col_r.at[slot], to)
        return carry

    lax.fori_loop(1, 2 * nz, send_column, 0)

    send(tbuf.at[2], tbuf.at[4], text_s.at[0], text_r.at[4], ring(-2))
    far = jnp.where(c == 0, -3, 1)
    send(tbuf.at[2], tbuf.at[2 - far], text_s.at[1], text_r.at[2 - far], ring(far))
    send(tbuf.at[2], tbuf.at[0], text_s.at[2], text_r.at[0], ring(2))
    to_sib = 1 + 2 * c
    send(tbuf.at[2], tbuf.at[to_sib], text_s.at[3], text_r.at[to_sib], sib)
    send(pool2.at[c], pool2.at[c], pair_s.at[0], pair_r.at[0], sib)

    j = lax.broadcasted_iota(jnp.int32, (kw, count), 0)
    a = lax.broadcasted_iota(jnp.int32, (kw, count), 1)
    pick_a = j == 3 * ((a // rows) * nz + a % nz) + 2 * ((a // nz) % 2)
    pick_a = pick_a.astype(F32).astype(BF16)
    jb = lax.broadcasted_iota(jnp.int32, (kw, chips), 0)
    kb = lax.broadcasted_iota(jnp.int32, (kw, chips), 1)
    pick_b = (jb == 3 * kb + 1).astype(F32).astype(BF16)
    own_pooled = pooled_ref[...]
    qmat[:, :count] = dot(own_pooled, pick_a).astype(BF16)
    qmat[:, count:] = dot(own_pooled, pick_b).astype(BF16)

    def wait_column(i, carry):
        other = ((c + i) % 2) * nz + (z + i // 2) % nz
        wait(column.at[other], col_r.at[other])
        return carry

    lax.fori_loop(1, 2 * nz, wait_column, 0)
    turn_a = lax.broadcasted_iota(jnp.int32, (16 * rows, 16 * rows), 0)
    turn_b = lax.broadcasted_iota(jnp.int32, (16 * rows, 16 * rows), 1)
    turn = ((turn_a // rows == turn_b % 16) & (turn_a % rows == turn_b // 16)).astype(F32).astype(BF16)
    turned = dot(turn, column[...].reshape(16 * rows, LANES))
    even = [turned[r * rows : r * rows + nz] for r in range(TILES)]
    odd = [pltpu.roll(turned[r * rows + nz : (r + 1) * rows], LANES // 2, 1) for r in range(TILES)]
    low = lax.broadcasted_iota(jnp.int32, (nz, LANES), 1) < LANES // 2
    tiles = [jnp.concatenate([even[b], jnp.where(low, odd[4 + b], odd[5 + b])], axis=0) for b in range(9)]
    middle = even[9:13] + [jnp.where(low, even[13], odd[0])]
    middle += [jnp.where(low, odd[b - 5], odd[b - 4]) for b in range(5, 9)] + [jnp.zeros((nz, LANES), F32)]
    tiles += [jnp.concatenate([middle[b], middle[5 + b]], axis=0) for b in range(5)]
    here = pl.multiple_of((x * ny + y) * rows, rows)
    for t in range(7):
        wbuf[c, pl.ds(here, rows), t * LANES : (t + 1) * LANES] = jnp.where(
            c == 0, tiles[t], tiles[7 + t]
        ).astype(BF16)

    def block(xx, yy):
        return wbuf.at[c, pl.ds(pl.multiple_of((xx * ny + yy) * rows, rows), rows), :]

    def share_x(yy, k):
        for d in xdist:
            send(block(x, yy), block(x, yy), wx_s.at[k, d], wx_r.at[x, yy], device((x + d) % nx, y, z, c))

    for d in ydist:
        send(block(x, y), block(x, y), wy_s.at[d], wy_r.at[y], device(x, (y + d) % ny, z, c))
    share_x(y, 0)
    for d in ydist:
        yy = (y + d) % ny
        wait(block(x, yy), wy_r.at[yy])
        share_x(yy, d)

    def whole(core, xx):
        return wbuf.at[core, pl.ds(pl.multiple_of(xx * span, span), span), :]

    send(whole(c, x), whole(c, x), wsib_s.at[0], wsib_r.at[x], sib)

    wait(pool2.at[1 - c], pair_r.at[0])
    jt = lax.broadcasted_iota(jnp.int32, (chips, kw), 1)
    kt = lax.broadcasted_iota(jnp.int32, (chips, kw), 0)
    both = pool2[...].reshape(2 * tok, kw)
    pat[...] = dot_t((jt == 3 * kt + 2 * c).astype(F32).astype(BF16), both).astype(BF16)
    pbt[...] = dot_t((jt == 3 * kt + 1).astype(F32).astype(BF16), both).astype(BF16)

    wait(tbuf.at[4], text_r.at[4])
    pass_to = 3 + 2 * c
    send(tbuf.at[4], tbuf.at[pass_to], text_s.at[4], text_r.at[pass_to], sib)

    for d in xdist:
        xx = (x + d) % nx
        for yy in range(ny):
            wait(block(xx, yy), wx_r.at[xx, yy])
        send(whole(c, xx), whole(c, xx), wsib_s.at[d], wsib_r.at[xx], sib)
    for d in [0] + xdist:
        xx = (x + d) % nx
        wait(whole(1 - c, xx), wsib_r.at[xx])

    packed = wbuf[1, :, 2 * LANES :].astype(F32).reshape(nx * ny, rows, 5 * LANES)
    bpart[:, : 5 * LANES] = packed[:, :nz].reshape(chips, 5 * LANES).astype(BF16)
    bpart[:, 5 * LANES :] = packed[:, nz:, : 4 * LANES].reshape(chips, 4 * LANES).astype(BF16)

    qa, qb = qmat[:, :count], qmat[:, count:]
    image = jnp.concatenate(
        [
            dot(qa, wbuf[0]) + dot(qb, bpart[:, :HALF]),
            dot(qa, wbuf[1, :, : 2 * LANES]) + dot(qb, bpart[:, HALF:]),
        ],
        axis=1,
    ) + other_ref[...].astype(F32)
    image_inv = 1.0 / jnp.sqrt(jnp.sum(image * image, axis=1, keepdims=True) + EPS)
    image_unit = image * image_inv
    ibuf[3] = image_unit.astype(BF16)

    send(ibuf.at[3], ibuf.at[1], img_s.at[0], img_r.at[1], ring(2))
    afar = jnp.where(c == 1, 3, -1)
    send(ibuf.at[3], ibuf.at[3 - afar], img_s.at[1], img_r.at[3 - afar], ring(afar))
    send(ibuf.at[3], ibuf.at[5], img_s.at[2], img_r.at[5], ring(-2))
    img_sib = 2 + 2 * c
    send(ibuf.at[3], ibuf.at[img_sib], img_s.at[3], img_r.at[img_sib], sib)

    temper = jnp.exp(jnp.full((1, 1), scale_ref[0], F32))
    bias = bias_ref[0]
    row = lax.broadcasted_iota(jnp.int32, (tok, WINDOW * tok), 0)
    col = lax.broadcasted_iota(jnp.int32, (tok, WINDOW * tok), 1)

    def pairs(unit, blocks, own):
        logits = temper * dot_t(unit, blocks) + bias
        sign = jnp.where(col == row + own * tok, -1.0, 1.0)
        coef = (temper * sign / (1.0 + jnp.exp(-sign * logits))).astype(BF16)
        return dot(coef, blocks)

    for k in (0, 1, 3, 5):
        wait(tbuf.at[k], text_r.at[k])
    emb_grad = pairs(ibuf[3], tbuf[...].reshape(WINDOW * tok, D), 2)
    image_grad = (
        (emb_grad - image_unit * jnp.sum(image_unit * emb_grad, axis=1, keepdims=True)) * image_inv
    ).astype(BF16)
    grad2[c] = image_grad
    send(grad2.at[c], grad2.at[c], pair_s.at[1], pair_r.at[1], sib)

    wait(grad2.at[1 - c], pair_r.at[1])
    grads = grad2[...].reshape(2 * tok, D)
    side = jnp.where(c == 0, grads[:, : 5 * LANES], grads[:, 4 * LANES :])

    def term(xx):
        at = pl.ds(pl.multiple_of(xx * ny * nz, ny * nz), ny * nz)
        full = dot(pat[at, :], grads)
        tail = dot(pbt[at, :], side)
        top = full[:, :HALF].reshape(ny, nz, HALF)
        end = jnp.concatenate([full[:, HALF:], tail], axis=1).reshape(ny, nz, HALF)
        return jnp.concatenate([top, end], axis=1)

    for d in xdist[::-1]:
        xx = (x + d) % nx
        gsend[d] = term(xx).astype(BF16)
        for e in ydist + [0]:
            yy = (y + e) % ny
            send(gsend.at[d, yy], grecv.at[x, yy], gx_s.at[d, yy], gx_r.at[x, yy], device(xx, y, z, c))
    gown[...] = term(x)

    wait(ibuf.at[1], img_r.at[1])
    img_pass = 2 * c
    send(ibuf.at[1], ibuf.at[img_pass], img_s.at[4], img_r.at[img_pass], sib)

    def sum_x(yy):
        total = gown[yy]
        for d in xdist:
            xx = (x + d) % nx
            wait(grecv.at[xx, yy], gx_r.at[xx, yy])
            total += grecv[xx, yy].astype(F32)
        return total

    for e in ydist:
        yy = (y + e) % ny
        ysend[yy] = sum_x(yy).astype(BF16)
        send(ysend.at[yy], yrecv.at[y], gy_s.at[yy], gy_r.at[y], device(x, yy, z, c))
    yown[...] = sum_x(y)

    own_grad = grad2[c]
    to_a = dot_t(own_grad[:, :HALF], wbuf[0]) + dot_t(own_grad[:, HALF:], wbuf[1, :, : 2 * LANES])
    to_b = dot_t(own_grad, bpart[...])
    pooled_grad_ref[...] = (dot_t(to_a.astype(BF16), pick_a) + dot_t(to_b.astype(BF16), pick_b)).astype(BF16)

    total = yown[...]
    for e in ydist:
        yy = (y + e) % ny
        wait(yrecv.at[yy], gy_r.at[yy])
        total += yrecv[yy].astype(F32)
    zsend[...] = jnp.zeros_like(zsend)
    for t in range(TILES):
        part = total[:nz] if t < 7 else total[nz:]
        zsend[pl.ds(t, nz, stride=16), :] = part[:, (t % 7) * LANES : (t % 7 + 1) * LANES]

    def zrow(zz):
        return zsend.at[pl.ds(pl.multiple_of(zz * 16, 16), 16), :]

    for e in ring_order(nz):
        zz = (z + e) % nz
        send(zrow(zz), zrecv.at[z], gz_s.at[zz], gz_r.at[z], device(x, y, zz, c))

    for k in (0, 2, 4, 5):
        wait(ibuf.at[k], img_r.at[k])
    text_emb_grad = pairs(tbuf[2], ibuf[...].reshape(WINDOW * tok, D), 3)
    text_again = text_ref[...].astype(F32)
    again_inv = 1.0 / jnp.sqrt(jnp.sum(text_again * text_again, axis=1, keepdims=True) + EPS)
    text_unit = text_again * again_inv
    text_grad_ref[...] = (
        text_emb_grad - text_unit * jnp.sum(text_unit * text_emb_grad, axis=1, keepdims=True)
    ) * again_inv

    summed = zsend[pl.ds(pl.multiple_of(z * 16, 16), 16), :]
    for e in ring_order(nz):
        zz = (z + e) % nz
        wait(zrecv.at[zz], gz_r.at[zz])
        summed += zrecv[zz]
    weight_grad_ref[...] = summed

    def sent_column(i, carry):
        wait(column.at[slot], col_s.at[i])
        return carry

    lax.fori_loop(1, 2 * nz, sent_column, 0)
    for k in range(5):
        wait(tbuf.at[2], text_s.at[k])
        wait(ibuf.at[3], img_s.at[k])
    wait(pool2.at[c], pair_s.at[0])
    wait(grad2.at[c], pair_s.at[1])
    for d in ydist:
        wait(block(x, y), wy_s.at[d])
    for d in xdist:
        for k in range(ny):
            wait(block(x, y), wx_s.at[k, d])
            wait(gsend.at[d, k], gx_s.at[d, k])
    for d in [0] + xdist:
        wait(whole(c, x), wsib_s.at[d])
    for e in ydist:
        yy = (y + e) % ny
        wait(ysend.at[yy], gy_s.at[yy])
    for e in ring_order(nz):
        zz = (z + e) % nz
        wait(zrow(zz), gz_s.at[zz])


def body(dims, pooled, other_part, head_weight, text, logit_scale, logit_bias):
    nx, ny, nz = dims
    count = 2 * nx * ny * nz
    tok, kw = pooled.shape
    rows = 2 * nz
    dma = lambda *shape: pltpu.SemaphoreType.DMA(shape)
    vmem = pl.BlockSpec(memory_space=pltpu.VMEM)
    smem = pl.BlockSpec(memory_space=pltpu.SMEM)
    pooled_grad, text_grad, total = pl.pallas_call(
        functools.partial(kernel, dims),
        out_shape=(
            jax.ShapeDtypeStruct((tok, kw), BF16),
            jax.ShapeDtypeStruct((tok, D), F32),
            jax.ShapeDtypeStruct((16, LANES), F32),
        ),
        in_specs=[vmem, vmem, vmem, vmem, smem, smem],
        out_specs=(vmem, vmem, vmem),
        scratch_shapes=[
            pltpu.VMEM((16, LANES), F32),
            pltpu.VMEM((rows, 16, LANES), BF16),
            pltpu.VMEM((2, count, HALF), BF16),
            pltpu.VMEM((count // 2, D), BF16),
            pltpu.VMEM((WINDOW, tok, D), BF16),
            pltpu.VMEM((WINDOW, tok, D), BF16),
            pltpu.VMEM((2, tok, kw), BF16),
            pltpu.VMEM((2, tok, D), BF16),
            pltpu.VMEM((tok, kw), BF16),
            pltpu.VMEM((count // 2, 2 * tok), BF16),
            pltpu.VMEM((count // 2, 2 * tok), BF16),
            pltpu.VMEM((nx, ny, rows, HALF), BF16),
            pltpu.VMEM((ny, rows, HALF), F32),
            pltpu.VMEM((nx, ny, rows, HALF), BF16),
            pltpu.VMEM((ny, rows, HALF), BF16),
            pltpu.VMEM((rows, HALF), F32),
            pltpu.VMEM((ny, rows, HALF), BF16),
            pltpu.VMEM((nz * 16, LANES), F32),
            pltpu.VMEM((nz, 16, LANES), F32),
            dma(rows), dma(rows),
            dma(ny), dma(ny),
            dma(ny, nx), dma(nx, ny),
            dma(nx), dma(nx),
            dma(5), dma(WINDOW),
            dma(5), dma(WINDOW),
            dma(2), dma(2),
            dma(nx, ny), dma(nx, ny),
            dma(ny), dma(ny),
            dma(nz), dma(nz),
        ],
        compiler_params=pltpu.CompilerParams(
            collective_id=0, has_side_effects=True, vmem_limit_bytes=48 * 1024 * 1024
        ),
    )(pooled, other_part, head_weight, text, logit_scale, logit_bias)
    flat = total[:TILES].reshape(1, TILES * LANES)
    first = flat[:, :GROUP]
    second = jnp.concatenate([flat[:, D + 64 :], flat[:, :D]], axis=1)
    weight_grad = jnp.where(lax.axis_index("dp") % 2 == 0, first, second)
    return pooled_grad, text_grad, weight_grad


def solution(mesh, dims=(X, Y, Z)):
    return jax.shard_map(
        functools.partial(body, dims),
        mesh=mesh,
        in_specs=(P("dp", None), P("dp", None), P("dp", None), P("dp", None), P(), P()),
        out_specs=(P("dp", None), P("dp", None), P("dp", None)),
        check_vma=False,
    )
```

```python
import functools

import jax
import jax.numpy as jnp
from jax import lax
from jax.experimental import pallas as pl
from jax.experimental.pallas import tpu as pltpu
from jax.sharding import PartitionSpec as P

D = 1152
GROUP = 1728
LANES = 128
TILES = 14
HALF = 896
WINDOW = 6
X, Y, Z = 4, 8, 8
EPS = 1e-06
LAG = 2
BY_RIGHT = (0, 2, 4)
DIRECT = (5, 6, 7)
SUM_RIGHT = (3, 5)
SUM_NONE = (0, 1, 2)
F32 = jnp.float32
BF16 = jnp.bfloat16
MESH = pl.DeviceIdType.MESH


def dot(a, b):
    return jnp.dot(a, b, preferred_element_type=F32)


def dot_t(a, b):
    return lax.dot_general(a, b, (((1,), (1,)), ((), ())), preferred_element_type=F32)


def ring_order(n):
    return sorted(range(1, n), key=lambda d: (min(d, n - d), d))


def kernel(
    dims,
    pooled_hbm, other_hbm, shard_hbm, text_hbm, scale_ref, bias_ref,
    pooled_grad_ref, text_grad_ref, weight_grad_ref,
    pooled_ref, other_ref, shard_ref, text_ref,
    fold, column, wbuf, bpart, tbuf, ibuf, pool2, grad2, qmat, pat, pbt,
    gsend, gterm, gown, grecv, ysend, yown, yrecv, zsend, zrecv,
    col_s, col_r, wy_s, wy_r, wx_s, wx_r, wsib_s, wsib_r,
    text_s, text_r, img_s, img_r, pair_s, pair_r,
    gx_s, gx_r, gy_s, gy_r, gz_s, gz_r, load_sem,
):
    nx, ny, nz = dims
    count = nx * ny * nz * 2
    rows = 2 * nz
    span = ny * rows
    tok = pooled_ref.shape[0]
    kw = pooled_ref.shape[1]
    chips = count // 2

    me = lax.axis_index("dp")
    c = me % 2
    z = (me // 2) % nz
    y = (me // (2 * nz)) % ny
    x = me // (2 * nz * ny)
    sib = me + 1 - 2 * c

    def device(xx, yy, zz, cc):
        return ((xx * ny + yy) * nz + zz) * 2 + cc

    def ring(step):
        return (me + step + count) % count

    sent = []

    def send(src, dst, ssem, rsem, to):
        pltpu.make_async_remote_copy(
            src_ref=src, dst_ref=dst, send_sem=ssem, recv_sem=rsem, device_id=(to,), device_id_type=MESH
        ).start()
        sent.append((src, ssem))

    def wait(ref, sem):
        pltpu.make_async_copy(ref, ref, sem).wait()

    loads = [
        pltpu.make_async_copy(src, dst, load_sem.at[k])
        for k, (src, dst) in enumerate(
            [(shard_hbm, shard_ref), (text_hbm, text_ref), (pooled_hbm, pooled_ref), (other_hbm, other_ref)]
        )
    ]
    ydist = ring_order(ny)
    xdist = ring_order(nx)

    barrier = pltpu.get_barrier_semaphore()

    def hello(to):
        pl.semaphore_signal(barrier, inc=1, device_id=(to,), device_id_type=MESH)

    def hello_column(i, carry):
        hello(device(x, y, (z + i // 2) % nz, (c + i) % 2))
        return carry

    lax.fori_loop(1, 2 * nz, hello_column, 0)
    for d in ydist:
        hello(device(x, (y + d) % ny, z, c))
    for d in xdist:
        hello(device((x + d) % nx, y, z, c))
    for d in (-3, -2, -1, 1, 2, 3):
        hello(ring(d))

    for load in loads:
        load.start()

    loads[0].wait()
    piece = shard_ref[...].astype(F32)
    fold[...] = jnp.zeros_like(fold)
    for r in range(TILES - 1):
        fold[r : r + 1, :] = piece[:, r * LANES : (r + 1) * LANES]
    fold[TILES - 1 : TILES, : LANES // 2] = piece[:, (TILES - 1) * LANES :]
    slot = c * nz + z
    column[slot] = fold[...].astype(BF16)

    loads[1].wait()
    text = text_ref[...].astype(F32)
    text_inv = 1.0 / jnp.sqrt(jnp.sum(text * text, axis=1, keepdims=True) + EPS)
    tbuf[2] = (text * text_inv).astype(BF16)
    loads[2].wait()
    pool2[c] = pooled_ref[...]

    pl.semaphore_wait(barrier, 2 * nz - 1 + len(ydist) + len(xdist) + 6)

    for i in range(1, 2 * nz):
        to = device(x, y, (z + i // 2) % nz, (c + i) % 2)
        send(column.at[slot], column.at[slot], col_s.at[i], col_r.at[slot], to)

    send(pool2.at[c], pool2.at[c], pair_s.at[0], pair_r.at[0], sib)

    j = lax.broadcasted_iota(jnp.int32, (kw, count), 0)
    a = lax.broadcasted_iota(jnp.int32, (kw, count), 1)
    pick_a = j == 3 * ((a // rows) * nz + a % nz) + 2 * ((a // nz) % 2)
    pick_a = pick_a.astype(F32).astype(BF16)
    jb = lax.broadcasted_iota(jnp.int32, (kw, chips), 0)
    kb = lax.broadcasted_iota(jnp.int32, (kw, chips), 1)
    pick_b = (jb == 3 * kb + 1).astype(F32).astype(BF16)
    own_pooled = pooled_ref[...]
    qmat[:, :count] = dot(own_pooled, pick_a).astype(BF16)
    qmat[:, count:] = dot(own_pooled, pick_b).astype(BF16)

    def wait_column(i, carry):
        other = ((c + i) % 2) * nz + (z + i // 2) % nz
        wait(column.at[other], col_r.at[other])
        return carry

    lax.fori_loop(1, 2 * nz, wait_column, 0)
    turn_a = lax.broadcasted_iota(jnp.int32, (16 * rows, 16 * rows), 0)
    turn_b = lax.broadcasted_iota(jnp.int32, (16 * rows, 16 * rows), 1)
    turn = ((turn_a // rows == turn_b % 16) & (turn_a % rows == turn_b // 16)).astype(F32).astype(BF16)
    turned = dot(turn, column[...].reshape(16 * rows, LANES))
    even = [turned[r * rows : r * rows + nz] for r in range(TILES)]
    odd = [pltpu.roll(turned[r * rows + nz : (r + 1) * rows], LANES // 2, 1) for r in range(TILES)]
    low = lax.broadcasted_iota(jnp.int32, (nz, LANES), 1) < LANES // 2
    tiles = [jnp.concatenate([even[b], jnp.where(low, odd[4 + b], odd[5 + b])], axis=0) for b in range(9)]
    middle = even[9:13] + [jnp.where(low, even[13], odd[0])]
    middle += [jnp.where(low, odd[b - 5], odd[b - 4]) for b in range(5, 9)] + [jnp.zeros((nz, LANES), F32)]
    tiles += [jnp.concatenate([middle[b], middle[5 + b]], axis=0) for b in range(5)]
    here = pl.multiple_of((x * ny + y) * rows, rows)
    for t in range(7):
        wbuf[c, pl.ds(here, rows), t * LANES : (t + 1) * LANES] = jnp.where(
            c == 0, tiles[t], tiles[7 + t]
        ).astype(BF16)

    def block(xx, yy):
        return wbuf.at[c, pl.ds(pl.multiple_of((xx * ny + yy) * rows, rows), rows), :]

    right, left = (x + 1) % nx, (x + nx - 1) % nx
    far = (x + 2) % nx
    to_right, to_left, to_far = device(right, y, z, c), device(left, y, z, c), device(far, y, z, c)

    def share_x(yy, k):
        send(block(x, yy), block(x, yy), wx_s.at[k, 0], wx_r.at[x, yy], to_right)
        send(block(x, yy), block(x, yy), wx_s.at[k, 1], wx_r.at[x, yy], to_left)
        if k in DIRECT:
            send(block(x, yy), block(x, yy), wx_s.at[k, 2], wx_r.at[x, yy], to_far)

    def pass_x(k):
        yy = (y + yorder[k]) % ny
        wait(block(left, yy), wx_r.at[left, yy])
        wait(block(right, yy), wx_r.at[right, yy])
        if k in BY_RIGHT:
            send(block(left, yy), block(left, yy), wx_s.at[k, 2], wx_r.at[left, yy], to_right)
        elif k not in DIRECT:
            send(block(right, yy), block(right, yy), wx_s.at[k, 2], wx_r.at[right, yy], to_left)

    yorder = [0] + ydist
    for d in ydist:
        send(block(x, y), block(x, y), wy_s.at[d], wy_r.at[y], device(x, (y + d) % ny, z, c))
    share_x(y, 0)
    send(tbuf.at[2], tbuf.at[4], text_s.at[0], text_r.at[4], ring(-2))
    send(tbuf.at[2], tbuf.at[0], text_s.at[1], text_r.at[0], ring(2))
    to_sib = 1 + 2 * c
    send(tbuf.at[2], tbuf.at[to_sib], text_s.at[2], text_r.at[to_sib], sib)
    for k in range(1, ny):
        yy = (y + yorder[k]) % ny
        wait(block(x, yy), wy_r.at[yy])
        share_x(yy, k)
        if k >= LAG:
            pass_x(k - LAG)

    def whole(core, xx):
        return wbuf.at[core, pl.ds(pl.multiple_of(xx * span, span), span), :]

    send(whole(c, x), whole(c, x), wsib_s.at[0], wsib_r.at[x], sib)

    wait(pool2.at[1 - c], pair_r.at[0])
    jt = lax.broadcasted_iota(jnp.int32, (chips, kw), 1)
    kt = lax.broadcasted_iota(jnp.int32, (chips, kw), 0)
    both = pool2[...].reshape(2 * tok, kw)
    pat[...] = dot_t((jt == 3 * kt + 2 * c).astype(F32).astype(BF16), both).astype(BF16)
    pbt[...] = dot_t((jt == 3 * kt + 1).astype(F32).astype(BF16), both).astype(BF16)

    wait(tbuf.at[4], text_r.at[4])
    wait(tbuf.at[0], text_r.at[0])
    pass_to = 3 + 2 * c
    send(tbuf.at[4], tbuf.at[pass_to], text_s.at[3], text_r.at[pass_to], sib)
    pass_from, pass_back = 4 - 4 * c, 5 - 4 * c
    send(tbuf.at[pass_from], tbuf.at[pass_back], text_s.at[4], text_r.at[pass_back], ring(-1))

    for k in range(ny - LAG, ny):
        pass_x(k)
    send(whole(c, left), whole(c, left), wsib_s.at[1], wsib_r.at[left], sib)
    send(whole(c, right), whole(c, right), wsib_s.at[2], wsib_r.at[right], sib)
    for k in range(ny):
        yy = (y + yorder[k]) % ny
        wait(block(far, yy), wx_r.at[far, yy])
        send(block(far, yy), block(far, yy), wsib_s.at[3 + k], wsib_r.at[far], sib)
    for xx in (x, left, right, far):
        wait(whole(1 - c, xx), wsib_r.at[xx])

    packed = wbuf[1, :, 2 * LANES :].astype(F32).reshape(nx * ny, rows, 5 * LANES)
    bpart[:, : 5 * LANES] = packed[:, :nz].reshape(chips, 5 * LANES).astype(BF16)
    bpart[:, 5 * LANES :] = packed[:, nz:, : 4 * LANES].reshape(chips, 4 * LANES).astype(BF16)

    loads[3].wait()
    qa, qb = qmat[:, :count], qmat[:, count:]
    image = jnp.concatenate(
        [
            dot(qa, wbuf[0]) + dot(qb, bpart[:, :HALF]),
            dot(qa, wbuf[1, :, : 2 * LANES]) + dot(qb, bpart[:, HALF:]),
        ],
        axis=1,
    ) + other_ref[...].astype(F32)
    image_inv = 1.0 / jnp.sqrt(jnp.sum(image * image, axis=1, keepdims=True) + EPS)
    image_unit = image * image_inv
    ibuf[3] = image_unit.astype(BF16)

    send(ibuf.at[3], ibuf.at[1], img_s.at[0], img_r.at[1], ring(2))
    send(ibuf.at[3], ibuf.at[5], img_s.at[1], img_r.at[5], ring(-2))
    img_sib = 2 + 2 * c
    send(ibuf.at[3], ibuf.at[img_sib], img_s.at[2], img_r.at[img_sib], sib)

    temper = jnp.exp(jnp.full((1, 1), scale_ref[0], F32))
    bias = bias_ref[0]
    row = lax.broadcasted_iota(jnp.int32, (tok, WINDOW * tok), 0)
    col = lax.broadcasted_iota(jnp.int32, (tok, WINDOW * tok), 1)

    def pairs(unit, blocks, own):
        logits = temper * dot_t(unit, blocks) + bias
        sign = jnp.where(col == row + own * tok, -1.0, 1.0)
        coef = (temper * sign / (1.0 + jnp.exp(-sign * logits))).astype(BF16)
        return dot(coef, blocks)

    for k in (1, 3, 5):
        wait(tbuf.at[k], text_r.at[k])
    emb_grad = pairs(ibuf[3], tbuf[...].reshape(WINDOW * tok, D), 2)
    image_grad = (
        (emb_grad - image_unit * jnp.sum(image_unit * emb_grad, axis=1, keepdims=True)) * image_inv
    ).astype(BF16)
    grad2[c] = image_grad
    send(grad2.at[c], grad2.at[c], pair_s.at[1], pair_r.at[1], sib)

    wait(grad2.at[1 - c], pair_r.at[1])
    grads = grad2[...].reshape(2 * tok, D)
    side = jnp.where(c == 0, grads[:, : 5 * LANES], grads[:, 4 * LANES :])

    def term(xx):
        at = pl.ds(pl.multiple_of(xx * ny * nz, ny * nz), ny * nz)
        full = dot(pat[at, :], grads)
        tail = dot(pbt[at, :], side)
        top = full[:, :HALF].reshape(ny, nz, HALF)
        end = jnp.concatenate([full[:, HALF:], tail], axis=1).reshape(ny, nz, HALF)
        return jnp.concatenate([top, end], axis=1)

    gsend[0] = term(far).astype(BF16)
    eorder = ydist[::-1] + [0]
    for k, e in enumerate(eorder):
        yy = (y + e) % ny
        to = to_far if k in SUM_NONE else to_right if k in SUM_RIGHT else to_left
        send(gsend.at[0, yy], grecv.at[2, yy], gx_s.at[0, yy], gx_r.at[2, yy], to)
    gterm[0] = term(right)
    gterm[1] = term(left)
    for k, e in enumerate(eorder):
        yy = (y + e) % ny
        to_r, to_l = gterm[0, yy], gterm[1, yy]
        if k not in SUM_NONE:
            wait(grecv.at[2, yy], gx_r.at[2, yy])
            passed = grecv[2, yy].astype(F32)
            if k in SUM_RIGHT:
                to_r += passed
            else:
                to_l += passed
        gsend[1, yy] = to_r.astype(BF16)
        gsend[2, yy] = to_l.astype(BF16)
        send(gsend.at[1, yy], grecv.at[0, yy], gx_s.at[1, yy], gx_r.at[0, yy], to_right)
        send(gsend.at[2, yy], grecv.at[1, yy], gx_s.at[2, yy], gx_r.at[1, yy], to_left)
    gown[...] = term(x)

    wait(ibuf.at[1], img_r.at[1])
    wait(ibuf.at[5], img_r.at[5])
    img_pass = 2 * c
    send(ibuf.at[1], ibuf.at[img_pass], img_s.at[3], img_r.at[img_pass], sib)
    img_from, img_on = 5 - 4 * c, 4 - 4 * c
    send(ibuf.at[img_from], ibuf.at[img_on], img_s.at[4], img_r.at[img_on], ring(1))

    def sum_x(k, yy):
        total = gown[yy]
        for n in (0, 1, 2) if k in SUM_NONE else (0, 1):
            wait(grecv.at[n, yy], gx_r.at[n, yy])
            total += grecv[n, yy].astype(F32)
        return total

    for k, e in enumerate(eorder[:-1]):
        yy = (y + e) % ny
        ysend[yy] = sum_x(k, yy).astype(BF16)
        send(ysend.at[yy], yrecv.at[y], gy_s.at[yy], gy_r.at[y], device(x, yy, z, c))
    yown[...] = sum_x(ny - 1, y)

    own_grad = grad2[c]
    to_a = dot_t(own_grad[:, :HALF], wbuf[0]) + dot_t(own_grad[:, HALF:], wbuf[1, :, : 2 * LANES])
    to_b = dot_t(own_grad, bpart[...])
    pooled_grad_ref[...] = (dot_t(to_a.astype(BF16), pick_a) + dot_t(to_b.astype(BF16), pick_b)).astype(BF16)

    total = yown[...]
    for e in ydist:
        yy = (y + e) % ny
        wait(yrecv.at[yy], gy_r.at[yy])
        total += yrecv[yy].astype(F32)
    zsend[...] = jnp.zeros_like(zsend)
    for t in range(TILES):
        part = total[:nz] if t < 7 else total[nz:]
        zsend[pl.ds(t, nz, stride=16), :] = part[:, (t % 7) * LANES : (t % 7 + 1) * LANES]

    def zrow(zz):
        return zsend.at[pl.ds(pl.multiple_of(zz * 16, 16), 16), :]

    for e in ring_order(nz):
        zz = (z + e) % nz
        send(zrow(zz), zrecv.at[z], gz_s.at[zz], gz_r.at[z], device(x, y, zz, c))

    for k in (0, 2, 4):
        wait(ibuf.at[k], img_r.at[k])
    text_emb_grad = pairs(tbuf[2], ibuf[...].reshape(WINDOW * tok, D), 3)
    text_again = text_ref[...].astype(F32)
    again_inv = 1.0 / jnp.sqrt(jnp.sum(text_again * text_again, axis=1, keepdims=True) + EPS)
    text_unit = text_again * again_inv
    text_grad_ref[...] = (
        text_emb_grad - text_unit * jnp.sum(text_unit * text_emb_grad, axis=1, keepdims=True)
    ) * again_inv

    summed = zsend[pl.ds(pl.multiple_of(z * 16, 16), 16), :]
    for e in ring_order(nz):
        zz = (z + e) % nz
        wait(zrecv.at[zz], gz_r.at[zz])
        summed += zrecv[zz]
    weight_grad_ref[...] = summed

    for ref, sem in sent:
        wait(ref, sem)


def body(dims, pooled, other_part, head_weight, text, logit_scale, logit_bias):
    nx, ny, nz = dims
    count = 2 * nx * ny * nz
    tok, kw = pooled.shape
    rows = 2 * nz
    dma = lambda *shape: pltpu.SemaphoreType.DMA(shape)
    vmem = pl.BlockSpec(memory_space=pltpu.VMEM)
    hbm = pl.BlockSpec(memory_space=pltpu.HBM)
    smem = pl.BlockSpec(memory_space=pltpu.SMEM)
    pooled_grad, text_grad, total = pl.pallas_call(
        functools.partial(kernel, dims),
        out_shape=(
            jax.ShapeDtypeStruct((tok, kw), BF16),
            jax.ShapeDtypeStruct((tok, D), F32),
            jax.ShapeDtypeStruct((16, LANES), F32),
        ),
        in_specs=[hbm, hbm, hbm, hbm, smem, smem],
        out_specs=(vmem, vmem, vmem),
        scratch_shapes=[
            pltpu.VMEM((tok, kw), BF16),
            pltpu.VMEM((tok, D), BF16),
            pltpu.VMEM((1, GROUP), BF16),
            pltpu.VMEM((tok, D), BF16),
            pltpu.VMEM((16, LANES), F32),
            pltpu.VMEM((rows, 16, LANES), BF16),
            pltpu.VMEM((2, count, HALF), BF16),
            pltpu.VMEM((count // 2, D), BF16),
            pltpu.VMEM((WINDOW, tok, D), BF16),
            pltpu.VMEM((WINDOW, tok, D), BF16),
            pltpu.VMEM((2, tok, kw), BF16),
            pltpu.VMEM((2, tok, D), BF16),
            pltpu.VMEM((tok, kw), BF16),
            pltpu.VMEM((count // 2, 2 * tok), BF16),
            pltpu.VMEM((count // 2, 2 * tok), BF16),
            pltpu.VMEM((3, ny, rows, HALF), BF16),
            pltpu.VMEM((2, ny, rows, HALF), F32),
            pltpu.VMEM((ny, rows, HALF), F32),
            pltpu.VMEM((3, ny, rows, HALF), BF16),
            pltpu.VMEM((ny, rows, HALF), BF16),
            pltpu.VMEM((rows, HALF), F32),
            pltpu.VMEM((ny, rows, HALF), BF16),
            pltpu.VMEM((nz * 16, LANES), F32),
            pltpu.VMEM((nz, 16, LANES), F32),
            dma(rows), dma(rows),
            dma(ny), dma(ny),
            dma(ny, 3), dma(nx, ny),
            dma(3 + ny), dma(nx),
            dma(5), dma(WINDOW),
            dma(5), dma(WINDOW),
            dma(2), dma(2),
            dma(3, ny), dma(3, ny),
            dma(ny), dma(ny),
            dma(nz), dma(nz),
            dma(4),
        ],
        compiler_params=pltpu.CompilerParams(
            collective_id=0, has_side_effects=True, vmem_limit_bytes=60 * 1024 * 1024
        ),
    )(pooled, other_part, head_weight, text, logit_scale, logit_bias)
    flat = total[:TILES].reshape(1, TILES * LANES)
    first = flat[:, :GROUP]
    second = jnp.concatenate([flat[:, D + 64 :], flat[:, :D]], axis=1)
    weight_grad = jnp.where(lax.axis_index("dp") % 2 == 0, first, second)
    return pooled_grad, text_grad, weight_grad


def solution(mesh, dims=(X, Y, Z)):
    return jax.shard_map(
        functools.partial(body, dims),
        mesh=mesh,
        in_specs=(P("dp", None), P("dp", None), P("dp", None), P("dp", None), P(), P()),
        out_specs=(P("dp", None), P("dp", None), P("dp", None)),
        check_vma=False,
    )
```

```python
import functools

import jax
import jax.numpy as jnp
from jax import lax
from jax.experimental import pallas as pl
from jax.experimental.pallas import tpu as pltpu
from jax.sharding import PartitionSpec as P

D = 1152
GROUP = 1728
LANES = 128
TILES = 14
HALF = 896
WINDOW = 6
X, Y, Z = 4, 8, 8
EPS = 1e-06
LAG = 2
BY_RIGHT = (0, 2, 4)
DIRECT = (5, 6, 7)
SUM_RIGHT = (3, 5)
SUM_NONE = (0, 1, 2)
F32 = jnp.float32
BF16 = jnp.bfloat16
MESH = pl.DeviceIdType.MESH


def dot(a, b):
    return jnp.dot(a, b, preferred_element_type=F32)


def dot_t(a, b):
    return lax.dot_general(a, b, (((1,), (1,)), ((), ())), preferred_element_type=F32)


def ring_order(n):
    return sorted(range(1, n), key=lambda d: (min(d, n - d), d))


def kernel(
    dims,
    pooled_hbm, other_hbm, shard_hbm, text_hbm, scale_ref, bias_ref,
    pooled_grad_hbm, text_grad_hbm, weight_grad_hbm,
    pooled_ref, other_ref, shard_ref, text_ref, pooled_grad_ref, text_grad_ref, weight_grad_ref,
    fold, column, wbuf, bpart, tbuf, ibuf, pool2, grad2, qmat, pat, pbt,
    gsend, gterm, gown, grecv, ysend, yown, yrecv, zsend, zrecv,
    col_s, col_r, wy_s, wy_r, wx_s, wx_r, wsib_s, wsib_r,
    text_s, text_r, img_s, img_r, pair_s, pair_r,
    gx_s, gx_r, gy_s, gy_r, gz_s, gz_r, load_sem, store_sem, ends_s, ends_r,
):
    nx, ny, nz = dims
    count = nx * ny * nz * 2
    rows = 2 * nz
    span = ny * rows
    tok = pooled_ref.shape[0]
    kw = pooled_ref.shape[1]
    chips = count // 2

    me = lax.axis_index("dp")
    c = me % 2
    z = (me // 2) % nz
    y = (me // (2 * nz)) % ny
    x = me // (2 * nz * ny)
    sib = me + 1 - 2 * c

    def device(xx, yy, zz, cc):
        return ((xx * ny + yy) * nz + zz) * 2 + cc

    def ring(step):
        return (me + step + count) % count

    sent = []

    def send(src, dst, ssem, rsem, to):
        pltpu.make_async_remote_copy(
            src_ref=src, dst_ref=dst, send_sem=ssem, recv_sem=rsem, device_id=(to,), device_id_type=MESH
        ).start()
        sent.append((src, ssem))

    def wait(ref, sem):
        pltpu.make_async_copy(ref, ref, sem).wait()

    loads = [
        pltpu.make_async_copy(src, dst, load_sem.at[k])
        for k, (src, dst) in enumerate(
            [(shard_hbm, shard_ref), (text_hbm, text_ref), (pooled_hbm, pooled_ref), (other_hbm, other_ref)]
        )
    ]
    stores = [
        pltpu.make_async_copy(src, dst, store_sem.at[k])
        for k, (src, dst) in enumerate(
            [(pooled_grad_ref, pooled_grad_hbm), (text_grad_ref, text_grad_hbm), (weight_grad_ref, weight_grad_hbm)]
        )
    ]
    ydist = ring_order(ny)
    xdist = ring_order(nx)

    barrier = pltpu.get_barrier_semaphore()

    def hello(to):
        pl.semaphore_signal(barrier, inc=1, device_id=(to,), device_id_type=MESH)

    def hello_column(i, carry):
        hello(device(x, y, (z + i // 2) % nz, (c + i) % 2))
        return carry

    lax.fori_loop(1, 2 * nz, hello_column, 0)
    for d in ydist:
        hello(device(x, (y + d) % ny, z, c))
    for d in xdist:
        hello(device((x + d) % nx, y, z, c))
    for d in (-3, -2, -1, 1, 2, 3):
        hello(ring(d))

    for load in loads:
        load.start()

    loads[0].wait()
    piece = shard_ref[...].astype(F32)
    fold[...] = jnp.zeros_like(fold)
    for r in range(TILES - 1):
        fold[r : r + 1, :] = piece[:, r * LANES : (r + 1) * LANES]
    fold[TILES - 1 : TILES, : LANES // 2] = piece[:, (TILES - 1) * LANES :]
    slot = c * nz + z
    column[slot] = fold[...].astype(BF16)

    loads[1].wait()
    text = text_ref[...].astype(F32)
    text_inv = 1.0 / jnp.sqrt(jnp.sum(text * text, axis=1, keepdims=True) + EPS)
    tbuf[2] = (text * text_inv).astype(BF16)
    loads[2].wait()
    pool2[c] = pooled_ref[...]

    pl.semaphore_wait(barrier, 2 * nz - 1 + len(ydist) + len(xdist) + 6)

    for i in range(1, 2 * nz):
        to = device(x, y, (z + i // 2) % nz, (c + i) % 2)
        send(column.at[slot], column.at[slot], col_s.at[i], col_r.at[slot], to)

    send(pool2.at[c], pool2.at[c], pair_s.at[0], pair_r.at[0], sib)

    j = lax.broadcasted_iota(jnp.int32, (kw, count), 0)
    a = lax.broadcasted_iota(jnp.int32, (kw, count), 1)
    pick_a = j == 3 * ((a // rows) * nz + a % nz) + 2 * ((a // nz) % 2)
    pick_a = pick_a.astype(F32).astype(BF16)
    jb = lax.broadcasted_iota(jnp.int32, (kw, chips), 0)
    kb = lax.broadcasted_iota(jnp.int32, (kw, chips), 1)
    pick_b = (jb == 3 * kb + 1).astype(F32).astype(BF16)
    own_pooled = pooled_ref[...]
    qmat[:, :count] = dot(own_pooled, pick_a).astype(BF16)
    qmat[:, count:] = dot(own_pooled, pick_b).astype(BF16)

    def wait_column(i, carry):
        other = ((c + i) % 2) * nz + (z + i // 2) % nz
        wait(column.at[other], col_r.at[other])
        return carry

    lax.fori_loop(1, 2 * nz, wait_column, 0)
    turn_a = lax.broadcasted_iota(jnp.int32, (16 * rows, 16 * rows), 0)
    turn_b = lax.broadcasted_iota(jnp.int32, (16 * rows, 16 * rows), 1)
    turn = ((turn_a // rows == turn_b % 16) & (turn_a % rows == turn_b // 16)).astype(F32).astype(BF16)
    turned = dot(turn, column[...].reshape(16 * rows, LANES))
    even = [turned[r * rows : r * rows + nz] for r in range(TILES)]
    odd = [pltpu.roll(turned[r * rows + nz : (r + 1) * rows], LANES // 2, 1) for r in range(TILES)]
    low = lax.broadcasted_iota(jnp.int32, (nz, LANES), 1) < LANES // 2
    tiles = [jnp.concatenate([even[b], jnp.where(low, odd[4 + b], odd[5 + b])], axis=0) for b in range(9)]
    middle = even[9:13] + [jnp.where(low, even[13], odd[0])]
    middle += [jnp.where(low, odd[b - 5], odd[b - 4]) for b in range(5, 9)] + [jnp.zeros((nz, LANES), F32)]
    tiles += [jnp.concatenate([middle[b], middle[5 + b]], axis=0) for b in range(5)]
    here = pl.multiple_of((x * ny + y) * rows, rows)
    for t in range(7):
        wbuf[c, pl.ds(here, rows), t * LANES : (t + 1) * LANES] = jnp.where(
            c == 0, tiles[t], tiles[7 + t]
        ).astype(BF16)

    def block(xx, yy):
        return wbuf.at[c, pl.ds(pl.multiple_of((xx * ny + yy) * rows, rows), rows), :]

    right, left = (x + 1) % nx, (x + nx - 1) % nx
    far = (x + 2) % nx
    to_right, to_left, to_far = device(right, y, z, c), device(left, y, z, c), device(far, y, z, c)

    def share_x(yy, k):
        send(block(x, yy), block(x, yy), wx_s.at[k, 0], wx_r.at[x, yy], to_right)
        send(block(x, yy), block(x, yy), wx_s.at[k, 1], wx_r.at[x, yy], to_left)
        if k in DIRECT:
            send(block(x, yy), block(x, yy), wx_s.at[k, 2], wx_r.at[x, yy], to_far)

    def pass_x(k):
        yy = (y + yorder[k]) % ny
        wait(block(left, yy), wx_r.at[left, yy])
        wait(block(right, yy), wx_r.at[right, yy])
        if k in DIRECT:
            pass
        elif k in BY_RIGHT:
            send(block(left, yy), block(left, yy), wx_s.at[k, 2], wx_r.at[left, yy], to_right)
        else:
            send(block(right, yy), block(right, yy), wx_s.at[k, 2], wx_r.at[right, yy], to_left)

    yorder = [0] + ydist
    for d in ydist:
        send(block(x, y), block(x, y), wy_s.at[d], wy_r.at[y], device(x, (y + d) % ny, z, c))
    share_x(y, 0)
    send(tbuf.at[2], tbuf.at[4], text_s.at[0], text_r.at[4], ring(-2))
    send(tbuf.at[2], tbuf.at[0], text_s.at[1], text_r.at[0], ring(2))
    to_sib = 1 + 2 * c
    send(tbuf.at[2], tbuf.at[to_sib], text_s.at[2], text_r.at[to_sib], sib)
    for k in range(1, ny):
        yy = (y + yorder[k]) % ny
        wait(block(x, yy), wy_r.at[yy])
        share_x(yy, k)
        if k >= LAG:
            pass_x(k - LAG)

    def whole(core, xx):
        return wbuf.at[core, pl.ds(pl.multiple_of(xx * span, span), span), :]

    send(whole(c, x), whole(c, x), wsib_s.at[0], wsib_r.at[x], sib)

    wait(pool2.at[1 - c], pair_r.at[0])
    jt = lax.broadcasted_iota(jnp.int32, (chips, kw), 1)
    kt = lax.broadcasted_iota(jnp.int32, (chips, kw), 0)
    both = pool2[...].reshape(2 * tok, kw)
    pat[...] = dot_t((jt == 3 * kt + 2 * c).astype(F32).astype(BF16), both).astype(BF16)
    pbt[...] = dot_t((jt == 3 * kt + 1).astype(F32).astype(BF16), both).astype(BF16)

    wait(tbuf.at[4], text_r.at[4])
    wait(tbuf.at[0], text_r.at[0])
    pass_to = 3 + 2 * c
    send(tbuf.at[4], tbuf.at[pass_to], text_s.at[3], text_r.at[pass_to], sib)
    pass_from, pass_back = 4 - 4 * c, 5 - 4 * c
    send(tbuf.at[pass_from], tbuf.at[pass_back], text_s.at[4], text_r.at[pass_back], ring(-1))

    for k in range(ny - LAG, ny):
        pass_x(k)
    send(whole(c, left), whole(c, left), wsib_s.at[1], wsib_r.at[left], sib)
    send(whole(c, right), whole(c, right), wsib_s.at[2], wsib_r.at[right], sib)
    for k in range(ny):
        yy = (y + yorder[k]) % ny
        wait(block(far, yy), wx_r.at[far, yy])
        send(block(far, yy), block(far, yy), wsib_s.at[3 + k], wsib_r.at[far], sib)
    for xx in (x, left, right, far):
        wait(whole(1 - c, xx), wsib_r.at[xx])

    packed = wbuf[1, :, 2 * LANES :].astype(F32).reshape(nx * ny, rows, 5 * LANES)
    bpart[:, : 5 * LANES] = packed[:, :nz].reshape(chips, 5 * LANES).astype(BF16)
    bpart[:, 5 * LANES :] = packed[:, nz:, : 4 * LANES].reshape(chips, 4 * LANES).astype(BF16)

    loads[3].wait()
    qa, qb = qmat[:, :count], qmat[:, count:]
    image = jnp.concatenate(
        [
            dot(qa, wbuf[0]) + dot(qb, bpart[:, :HALF]),
            dot(qa, wbuf[1, :, : 2 * LANES]) + dot(qb, bpart[:, HALF:]),
        ],
        axis=1,
    ) + other_ref[...].astype(F32)
    image_inv = 1.0 / jnp.sqrt(jnp.sum(image * image, axis=1, keepdims=True) + EPS)
    image_unit = image * image_inv
    ibuf[3] = image_unit.astype(BF16)

    send(ibuf.at[3], ibuf.at[1], img_s.at[0], img_r.at[1], ring(2))
    send(ibuf.at[3], ibuf.at[5], img_s.at[1], img_r.at[5], ring(-2))
    img_sib = 2 + 2 * c
    send(ibuf.at[3], ibuf.at[img_sib], img_s.at[2], img_r.at[img_sib], sib)

    temper = jnp.exp(jnp.full((1, 1), scale_ref[0], F32))
    bias = bias_ref[0]
    row = lax.broadcasted_iota(jnp.int32, (tok, WINDOW * tok), 0)
    col = lax.broadcasted_iota(jnp.int32, (tok, WINDOW * tok), 1)

    def pairs(unit, blocks, own):
        logits = temper * dot_t(unit, blocks) + bias
        sign = jnp.where(col == row + own * tok, -1.0, 1.0)
        coef = (temper * sign / (1.0 + jnp.exp(-sign * logits))).astype(BF16)
        return dot(coef, blocks)

    for k in (1, 3, 5):
        wait(tbuf.at[k], text_r.at[k])
    emb_grad = pairs(ibuf[3], tbuf[...].reshape(WINDOW * tok, D), 2)
    image_grad = (
        (emb_grad - image_unit * jnp.sum(image_unit * emb_grad, axis=1, keepdims=True)) * image_inv
    ).astype(BF16)
    grad2[c] = image_grad
    send(grad2.at[c], grad2.at[c], pair_s.at[1], pair_r.at[1], sib)

    wait(grad2.at[1 - c], pair_r.at[1])
    grads = grad2[...].reshape(2 * tok, D)
    side = jnp.where(c == 0, grads[:, : 5 * LANES], grads[:, 4 * LANES :])

    def term(xx):
        at = pl.ds(pl.multiple_of(xx * ny * nz, ny * nz), ny * nz)
        full = dot(pat[at, :], grads)
        tail = dot(pbt[at, :], side)
        top = full[:, :HALF].reshape(ny, nz, HALF)
        end = jnp.concatenate([full[:, HALF:], tail], axis=1).reshape(ny, nz, HALF)
        return jnp.concatenate([top, end], axis=1)

    gsend[0] = term(far).astype(BF16)
    eorder = ydist[::-1] + [0]
    for k, e in enumerate(eorder):
        yy = (y + e) % ny
        to = to_far if k in SUM_NONE else to_right if k in SUM_RIGHT else to_left
        send(gsend.at[0, yy], grecv.at[2, yy], gx_s.at[0, yy], gx_r.at[2, yy], to)
    gterm[0] = term(right)
    gterm[1] = term(left)
    for k, e in enumerate(eorder):
        yy = (y + e) % ny
        to_r, to_l = gterm[0, yy], gterm[1, yy]
        if k not in SUM_NONE:
            wait(grecv.at[2, yy], gx_r.at[2, yy])
            passed = grecv[2, yy].astype(F32)
            if k in SUM_RIGHT:
                to_r += passed
            else:
                to_l += passed
        gsend[1, yy] = to_r.astype(BF16)
        gsend[2, yy] = to_l.astype(BF16)
        send(gsend.at[1, yy], grecv.at[0, yy], gx_s.at[1, yy], gx_r.at[0, yy], to_right)
        send(gsend.at[2, yy], grecv.at[1, yy], gx_s.at[2, yy], gx_r.at[1, yy], to_left)
    gown[...] = term(x)

    wait(ibuf.at[1], img_r.at[1])
    wait(ibuf.at[5], img_r.at[5])
    img_pass = 2 * c
    send(ibuf.at[1], ibuf.at[img_pass], img_s.at[3], img_r.at[img_pass], sib)
    img_from, img_on = 5 - 4 * c, 4 - 4 * c
    send(ibuf.at[img_from], ibuf.at[img_on], img_s.at[4], img_r.at[img_on], ring(1))

    def sum_x(k, yy):
        total = gown[yy]
        for n in (0, 1, 2) if k in SUM_NONE else (0, 1):
            wait(grecv.at[n, yy], gx_r.at[n, yy])
            total += grecv[n, yy].astype(F32)
        return total

    for k, e in enumerate(eorder[:-1]):
        yy = (y + e) % ny
        ysend[yy] = sum_x(k, yy).astype(BF16)
        send(ysend.at[yy], yrecv.at[y], gy_s.at[yy], gy_r.at[y], device(x, yy, z, c))
    yown[...] = sum_x(ny - 1, y)

    own_grad = grad2[c]
    to_a = dot_t(own_grad[:, :HALF], wbuf[0]) + dot_t(own_grad[:, HALF:], wbuf[1, :, : 2 * LANES])
    to_b = dot_t(own_grad, bpart[...])
    pooled_grad_ref[...] = (dot_t(to_a.astype(BF16), pick_a) + dot_t(to_b.astype(BF16), pick_b)).astype(BF16)

    stores[0].start()

    total = yown[...]
    for e in ydist:
        yy = (y + e) % ny
        wait(yrecv.at[yy], gy_r.at[yy])
        total += yrecv[yy].astype(F32)
    zsend[...] = jnp.zeros_like(zsend)
    for t in range(TILES):
        part = total[:nz] if t < 7 else total[nz:]
        zsend[pl.ds(t, nz, stride=16), :] = part[:, (t % 7) * LANES : (t % 7 + 1) * LANES]

    def zrow(zz):
        return zsend.at[pl.ds(pl.multiple_of(zz * 16, 16), 16), :]

    for e in ring_order(nz):
        zz = (z + e) % nz
        send(zrow(zz), zrecv.at[z], gz_s.at[zz], gz_r.at[z], device(x, y, zz, c))

    for k in (0, 2, 4):
        wait(ibuf.at[k], img_r.at[k])
    text_emb_grad = pairs(tbuf[2], ibuf[...].reshape(WINDOW * tok, D), 3)
    text_again = text_ref[...].astype(F32)
    again_inv = 1.0 / jnp.sqrt(jnp.sum(text_again * text_again, axis=1, keepdims=True) + EPS)
    text_unit = text_again * again_inv
    text_grad_ref[...] = (
        text_emb_grad - text_unit * jnp.sum(text_unit * text_emb_grad, axis=1, keepdims=True)
    ) * again_inv
    stores[1].start()

    summed = zsend[pl.ds(pl.multiple_of(z * 16, 16), 16), :]
    for e in ring_order(nz):
        zz = (z + e) % nz
        wait(zrecv.at[zz], gz_r.at[zz])
        summed += zrecv[zz]
    turned = pltpu.roll(summed, LANES // 2, 1)
    low = lax.broadcasted_iota(jnp.int32, (1, LANES), 1) < LANES // 2
    for b in range(TILES):
        first, second = (9 + b) % TILES, (10 + b) % TILES
        odd_row = jnp.where(low, turned[first : first + 1], turned[second : second + 1])
        row_b = jnp.where(c == 0, summed[b : b + 1], odd_row)
        width = min(LANES, GROUP - b * LANES)
        weight_grad_ref[:, b * LANES : b * LANES + width] = row_b[:, :width]
    stores[2].start()

    for ref, sem in sent:
        wait(ref, sem)
    for store in stores:
        store.wait()


def finish_kernel(a, b, c, a_out, b_out, c_out, a_held, b_held, c_held, in_sem, out_sem):
    parts = [(a, a_held, a_out), (b, b_held, b_out), (c, c_held, c_out)]
    loads = [pltpu.make_async_copy(src, held, in_sem.at[k]) for k, (src, held, _) in enumerate(parts)]
    stores = [pltpu.make_async_copy(held, dst, out_sem.at[k]) for k, (_, held, dst) in enumerate(parts)]
    for load in loads:
        load.start()
    for load, store in zip(loads, stores):
        load.wait()
        store.start()
    for store in stores:
        store.wait()


def body(dims, pooled, other_part, head_weight, text, logit_scale, logit_bias):
    nx, ny, nz = dims
    count = 2 * nx * ny * nz
    tok, kw = pooled.shape
    rows = 2 * nz
    dma = lambda *shape: pltpu.SemaphoreType.DMA(shape)
    hbm = pl.BlockSpec(memory_space=pltpu.HBM)
    smem = pl.BlockSpec(memory_space=pltpu.SMEM)
    made = pl.pallas_call(
        functools.partial(kernel, dims),
        out_shape=(
            jax.ShapeDtypeStruct((tok, kw), BF16),
            jax.ShapeDtypeStruct((tok, D), F32),
            jax.ShapeDtypeStruct((1, GROUP), F32),
        ),
        in_specs=[hbm, hbm, hbm, hbm, smem, smem],
        out_specs=(hbm, hbm, hbm),
        scratch_shapes=[
            pltpu.VMEM((tok, kw), BF16),
            pltpu.VMEM((tok, D), BF16),
            pltpu.VMEM((1, GROUP), BF16),
            pltpu.VMEM((tok, D), BF16),
            pltpu.VMEM((tok, kw), BF16),
            pltpu.VMEM((tok, D), F32),
            pltpu.VMEM((1, GROUP), F32),
            pltpu.VMEM((16, LANES), F32),
            pltpu.VMEM((rows, 16, LANES), BF16),
            pltpu.VMEM((2, count, HALF), BF16),
            pltpu.VMEM((count // 2, D), BF16),
            pltpu.VMEM((WINDOW, tok, D), BF16),
            pltpu.VMEM((WINDOW, tok, D), BF16),
            pltpu.VMEM((2, tok, kw), BF16),
            pltpu.VMEM((2, tok, D), BF16),
            pltpu.VMEM((tok, kw), BF16),
            pltpu.VMEM((count // 2, 2 * tok), BF16),
            pltpu.VMEM((count // 2, 2 * tok), BF16),
            pltpu.VMEM((3, ny, rows, HALF), BF16),
            pltpu.VMEM((2, ny, rows, HALF), F32),
            pltpu.VMEM((ny, rows, HALF), F32),
            pltpu.VMEM((3, ny, rows, HALF), BF16),
            pltpu.VMEM((ny, rows, HALF), BF16),
            pltpu.VMEM((rows, HALF), F32),
            pltpu.VMEM((ny, rows, HALF), BF16),
            pltpu.VMEM((nz * 16, LANES), F32),
            pltpu.VMEM((nz, 16, LANES), F32),
            dma(rows), dma(rows),
            dma(ny), dma(ny),
            dma(ny, 3), dma(nx, ny),
            dma(3 + ny), dma(nx),
            dma(5), dma(WINDOW),
            dma(5), dma(WINDOW),
            dma(2), dma(2),
            dma(3, ny), dma(3, ny),
            dma(ny), dma(ny),
            dma(nz), dma(nz),
            dma(4),
            dma(3),
            dma(4), dma(4),
        ],
        compiler_params=pltpu.CompilerParams(
            collective_id=0, has_side_effects=True, vmem_limit_bytes=60 * 1024 * 1024
        ),
    )(pooled, other_part, head_weight, text, logit_scale, logit_bias)
    return pl.pallas_call(
        finish_kernel,
        out_shape=tuple(jax.ShapeDtypeStruct(m.shape, m.dtype) for m in made),
        in_specs=[hbm, hbm, hbm],
        out_specs=(hbm, hbm, hbm),
        scratch_shapes=[pltpu.VMEM(m.shape, m.dtype) for m in made] + [dma(3), dma(3)],
        compiler_params=pltpu.CompilerParams(vmem_limit_bytes=60 * 1024 * 1024),
    )(*made)


def solution(mesh, dims=(X, Y, Z)):
    return jax.shard_map(
        functools.partial(body, dims),
        mesh=mesh,
        in_specs=(P("dp", None), P("dp", None), P("dp", None), P("dp", None), P(), P()),
        out_specs=(P("dp", None), P("dp", None), P("dp", None)),
        check_vma=False,
    )
```

```python
import functools

import jax
import jax.numpy as jnp
from jax import lax
from jax.experimental import pallas as pl
from jax.experimental.pallas import tpu as pltpu
from jax.sharding import PartitionSpec as P

D = 1152
GROUP = 1728
LANES = 128
TILES = 14
HALF = 896
WINDOW = 6
X, Y, Z = 4, 8, 8
EPS = 1e-06
LAG = 3
BY_RIGHT = (0, 2, 4)
DIRECT = (6, 7)
SUM_RIGHT = (3, 5, 7)
SUM_NONE = (0, 1)
F32 = jnp.float32
BF16 = jnp.bfloat16
MESH = pl.DeviceIdType.MESH


def dot(a, b):
    return jnp.dot(a, b, preferred_element_type=F32)


def dot_t(a, b):
    return lax.dot_general(a, b, (((1,), (1,)), ((), ())), preferred_element_type=F32)


def ring_order(n):
    return sorted(range(1, n), key=lambda d: (min(d, n - d), d))


def kernel(
    dims,
    pooled_hbm, other_hbm, shard_hbm, text_hbm, scale_ref, bias_ref,
    pooled_grad_hbm, text_grad_hbm, weight_grad_hbm,
    pooled_ref, other_ref, shard_ref, text_ref, pooled_grad_ref, text_grad_ref, weight_grad_ref,
    fold, column, wbuf, bpart, tbuf, ibuf, pool2, grad2, qmat, pat, pbt,
    gsend, gterm, gown, grecv, ysend, yown, yrecv, zsend, zrecv,
    col_s, col_r, wy_s, wy_r, wx_s, wx_r, wsib_s, wsib_r,
    text_s, text_r, img_s, img_r, pair_s, pair_r,
    gx_s, gx_r, gy_s, gy_r, gz_s, gz_r, load_sem, store_sem, ends_s, ends_r,
):
    nx, ny, nz = dims
    count = nx * ny * nz * 2
    rows = 2 * nz
    span = ny * rows
    tok = pooled_ref.shape[0]
    kw = pooled_ref.shape[1]
    chips = count // 2

    me = lax.axis_index("dp")
    c = me % 2
    z = (me // 2) % nz
    y = (me // (2 * nz)) % ny
    x = me // (2 * nz * ny)
    sib = me + 1 - 2 * c

    def device(xx, yy, zz, cc):
        return ((xx * ny + yy) * nz + zz) * 2 + cc

    def ring(step):
        return (me + step + count) % count

    sent = []

    def send(src, dst, ssem, rsem, to):
        pltpu.make_async_remote_copy(
            src_ref=src, dst_ref=dst, send_sem=ssem, recv_sem=rsem, device_id=(to,), device_id_type=MESH
        ).start()
        sent.append((src, ssem))

    def wait(ref, sem):
        pltpu.make_async_copy(ref, ref, sem).wait()

    loads = [
        pltpu.make_async_copy(src, dst, load_sem.at[k])
        for k, (src, dst) in enumerate(
            [(shard_hbm, shard_ref), (text_hbm, text_ref), (pooled_hbm, pooled_ref), (other_hbm, other_ref)]
        )
    ]
    stores = [
        pltpu.make_async_copy(src, dst, store_sem.at[k])
        for k, (src, dst) in enumerate(
            [(pooled_grad_ref, pooled_grad_hbm), (text_grad_ref, text_grad_hbm), (weight_grad_ref, weight_grad_hbm)]
        )
    ]
    ydist = ring_order(ny)
    xdist = ring_order(nx)

    barrier = pltpu.get_barrier_semaphore()

    def hello(to):
        pl.semaphore_signal(barrier, inc=1, device_id=(to,), device_id_type=MESH)

    def hello_column(i, carry):
        hello(device(x, y, (z + i // 2) % nz, (c + i) % 2))
        return carry

    lax.fori_loop(1, 2 * nz, hello_column, 0)
    for d in ydist:
        hello(device(x, (y + d) % ny, z, c))
    for d in xdist:
        hello(device((x + d) % nx, y, z, c))
    for d in (-3, -2, -1, 1, 2, 3):
        hello(ring(d))

    for load in loads:
        load.start()

    loads[0].wait()
    piece = shard_ref[...].astype(F32)
    fold[...] = jnp.zeros_like(fold)
    for r in range(TILES - 1):
        fold[r : r + 1, :] = piece[:, r * LANES : (r + 1) * LANES]
    fold[TILES - 1 : TILES, : LANES // 2] = piece[:, (TILES - 1) * LANES :]
    slot = c * nz + z
    column[slot] = fold[...].astype(BF16)

    loads[1].wait()
    text = text_ref[...].astype(F32)
    text_inv = 1.0 / jnp.sqrt(jnp.sum(text * text, axis=1, keepdims=True) + EPS)
    tbuf[2] = (text * text_inv).astype(BF16)
    loads[2].wait()
    pool2[c] = pooled_ref[...]

    pl.semaphore_wait(barrier, 2 * nz - 1 + len(ydist) + len(xdist) + 6)

    for i in range(1, 2 * nz):
        to = device(x, y, (z + i // 2) % nz, (c + i) % 2)
        send(column.at[slot], column.at[slot], col_s.at[i], col_r.at[slot], to)

    send(pool2.at[c], pool2.at[c], pair_s.at[0], pair_r.at[0], sib)

    j = lax.broadcasted_iota(jnp.int32, (kw, count), 0)
    a = lax.broadcasted_iota(jnp.int32, (kw, count), 1)
    pick_a = j == 3 * ((a // rows) * nz + a % nz) + 2 * ((a // nz) % 2)
    pick_a = pick_a.astype(F32).astype(BF16)
    jb = lax.broadcasted_iota(jnp.int32, (kw, chips), 0)
    kb = lax.broadcasted_iota(jnp.int32, (kw, chips), 1)
    pick_b = (jb == 3 * kb + 1).astype(F32).astype(BF16)
    own_pooled = pooled_ref[...]
    qmat[:, :count] = dot(own_pooled, pick_a).astype(BF16)
    qmat[:, count:] = dot(own_pooled, pick_b).astype(BF16)

    def wait_column(i, carry):
        other = ((c + i) % 2) * nz + (z + i // 2) % nz
        wait(column.at[other], col_r.at[other])
        return carry

    lax.fori_loop(1, 2 * nz, wait_column, 0)
    turn_a = lax.broadcasted_iota(jnp.int32, (16 * rows, 16 * rows), 0)
    turn_b = lax.broadcasted_iota(jnp.int32, (16 * rows, 16 * rows), 1)
    turn = ((turn_a // rows == turn_b % 16) & (turn_a % rows == turn_b // 16)).astype(F32).astype(BF16)
    turned = dot(turn, column[...].reshape(16 * rows, LANES))
    even = [turned[r * rows : r * rows + nz] for r in range(TILES)]
    odd = [pltpu.roll(turned[r * rows + nz : (r + 1) * rows], LANES // 2, 1) for r in range(TILES)]
    low = lax.broadcasted_iota(jnp.int32, (nz, LANES), 1) < LANES // 2
    tiles = [jnp.concatenate([even[b], jnp.where(low, odd[4 + b], odd[5 + b])], axis=0) for b in range(9)]
    middle = even[9:13] + [jnp.where(low, even[13], odd[0])]
    middle += [jnp.where(low, odd[b - 5], odd[b - 4]) for b in range(5, 9)] + [jnp.zeros((nz, LANES), F32)]
    tiles += [jnp.concatenate([middle[b], middle[5 + b]], axis=0) for b in range(5)]
    here = pl.multiple_of((x * ny + y) * rows, rows)
    for t in range(7):
        wbuf[c, pl.ds(here, rows), t * LANES : (t + 1) * LANES] = jnp.where(
            c == 0, tiles[t], tiles[7 + t]
        ).astype(BF16)

    def block(xx, yy):
        return wbuf.at[c, pl.ds(pl.multiple_of((xx * ny + yy) * rows, rows), rows), :]

    right, left = (x + 1) % nx, (x + nx - 1) % nx
    far = (x + 2) % nx
    to_right, to_left, to_far = device(right, y, z, c), device(left, y, z, c), device(far, y, z, c)

    def share_x(yy, k):
        send(block(x, yy), block(x, yy), wx_s.at[k, 0], wx_r.at[x, yy], to_right)
        send(block(x, yy), block(x, yy), wx_s.at[k, 1], wx_r.at[x, yy], to_left)
        if k in DIRECT:
            send(block(x, yy), block(x, yy), wx_s.at[k, 2], wx_r.at[x, yy], to_far)

    def pass_x(k):
        yy = (y + yorder[k]) % ny
        wait(block(left, yy), wx_r.at[left, yy])
        wait(block(right, yy), wx_r.at[right, yy])
        if k in DIRECT:
            pass
        elif k in BY_RIGHT:
            send(block(left, yy), block(left, yy), wx_s.at[k, 2], wx_r.at[left, yy], to_right)
        else:
            send(block(right, yy), block(right, yy), wx_s.at[k, 2], wx_r.at[right, yy], to_left)

    yorder = [0] + ydist
    for d in ydist:
        send(block(x, y), block(x, y), wy_s.at[d], wy_r.at[y], device(x, (y + d) % ny, z, c))
    share_x(y, 0)
    send(tbuf.at[2], tbuf.at[4], text_s.at[0], text_r.at[4], ring(-2))
    send(tbuf.at[2], tbuf.at[0], text_s.at[1], text_r.at[0], ring(2))
    to_sib = 1 + 2 * c
    send(tbuf.at[2], tbuf.at[to_sib], text_s.at[2], text_r.at[to_sib], sib)
    for k in range(1, ny):
        yy = (y + yorder[k]) % ny
        wait(block(x, yy), wy_r.at[yy])
        share_x(yy, k)
        if k >= LAG:
            pass_x(k - LAG)

    def whole(core, xx):
        return wbuf.at[core, pl.ds(pl.multiple_of(xx * span, span), span), :]

    send(whole(c, x), whole(c, x), wsib_s.at[0], wsib_r.at[x], sib)

    wait(pool2.at[1 - c], pair_r.at[0])
    jt = lax.broadcasted_iota(jnp.int32, (chips, kw), 1)
    kt = lax.broadcasted_iota(jnp.int32, (chips, kw), 0)
    both = pool2[...].reshape(2 * tok, kw)
    pat[...] = dot_t((jt == 3 * kt + 2 * c).astype(F32).astype(BF16), both).astype(BF16)
    pbt[...] = dot_t((jt == 3 * kt + 1).astype(F32).astype(BF16), both).astype(BF16)

    wait(tbuf.at[4], text_r.at[4])
    wait(tbuf.at[0], text_r.at[0])
    pass_to = 3 + 2 * c
    send(tbuf.at[4], tbuf.at[pass_to], text_s.at[3], text_r.at[pass_to], sib)
    pass_from, pass_back = 4 - 4 * c, 5 - 4 * c
    send(tbuf.at[pass_from], tbuf.at[pass_back], text_s.at[4], text_r.at[pass_back], ring(-1))

    for k in range(ny - LAG, ny):
        pass_x(k)
    send(whole(c, left), whole(c, left), wsib_s.at[1], wsib_r.at[left], sib)
    send(whole(c, right), whole(c, right), wsib_s.at[2], wsib_r.at[right], sib)
    for k in range(ny):
        yy = (y + yorder[k]) % ny
        wait(block(far, yy), wx_r.at[far, yy])
        send(block(far, yy), block(far, yy), wsib_s.at[3 + k], wsib_r.at[far], sib)
    for xx in (x, left, right, far):
        wait(whole(1 - c, xx), wsib_r.at[xx])

    packed = wbuf[1, :, 2 * LANES :].astype(F32).reshape(nx * ny, rows, 5 * LANES)
    bpart[:, : 5 * LANES] = packed[:, :nz].reshape(chips, 5 * LANES).astype(BF16)
    bpart[:, 5 * LANES :] = packed[:, nz:, : 4 * LANES].reshape(chips, 4 * LANES).astype(BF16)

    loads[3].wait()
    qa, qb = qmat[:, :count], qmat[:, count:]
    image = jnp.concatenate(
        [
            dot(qa, wbuf[0]) + dot(qb, bpart[:, :HALF]),
            dot(qa, wbuf[1, :, : 2 * LANES]) + dot(qb, bpart[:, HALF:]),
        ],
        axis=1,
    ) + other_ref[...].astype(F32)
    image_inv = 1.0 / jnp.sqrt(jnp.sum(image * image, axis=1, keepdims=True) + EPS)
    image_unit = image * image_inv
    ibuf[3] = image_unit.astype(BF16)

    send(ibuf.at[3], ibuf.at[1], img_s.at[0], img_r.at[1], ring(2))
    send(ibuf.at[3], ibuf.at[5], img_s.at[1], img_r.at[5], ring(-2))
    img_sib = 2 + 2 * c
    send(ibuf.at[3], ibuf.at[img_sib], img_s.at[2], img_r.at[img_sib], sib)

    temper = jnp.exp(jnp.full((1, 1), scale_ref[0], F32))
    bias = bias_ref[0]
    row = lax.broadcasted_iota(jnp.int32, (tok, WINDOW * tok), 0)
    col = lax.broadcasted_iota(jnp.int32, (tok, WINDOW * tok), 1)

    def pairs(unit, blocks, own):
        logits = temper * dot_t(unit, blocks) + bias
        sign = jnp.where(col == row + own * tok, -1.0, 1.0)
        coef = (temper * sign / (1.0 + jnp.exp(-sign * logits))).astype(BF16)
        return dot(coef, blocks)

    for k in (1, 3, 5):
        wait(tbuf.at[k], text_r.at[k])
    emb_grad = pairs(ibuf[3], tbuf[...].reshape(WINDOW * tok, D), 2)
    image_grad = (
        (emb_grad - image_unit * jnp.sum(image_unit * emb_grad, axis=1, keepdims=True)) * image_inv
    ).astype(BF16)
    grad2[c] = image_grad
    send(grad2.at[c], grad2.at[c], pair_s.at[1], pair_r.at[1], sib)

    wait(grad2.at[1 - c], pair_r.at[1])
    grads = grad2[...].reshape(2 * tok, D)
    side = jnp.where(c == 0, grads[:, : 5 * LANES], grads[:, 4 * LANES :])

    def term(xx):
        at = pl.ds(pl.multiple_of(xx * ny * nz, ny * nz), ny * nz)
        full = dot(pat[at, :], grads)
        tail = dot(pbt[at, :], side)
        top = full[:, :HALF].reshape(ny, nz, HALF)
        end = jnp.concatenate([full[:, HALF:], tail], axis=1).reshape(ny, nz, HALF)
        return jnp.concatenate([top, end], axis=1)

    gsend[0] = term(far).astype(BF16)
    eorder = ydist[::-1] + [0]
    for k, e in enumerate(eorder):
        yy = (y + e) % ny
        to = to_far if k in SUM_NONE else to_right if k in SUM_RIGHT else to_left
        send(gsend.at[0, yy], grecv.at[2, yy], gx_s.at[0, yy], gx_r.at[2, yy], to)
    gterm[0] = term(right)
    gterm[1] = term(left)
    for k, e in enumerate(eorder):
        yy = (y + e) % ny
        to_r, to_l = gterm[0, yy], gterm[1, yy]
        if k not in SUM_NONE:
            wait(grecv.at[2, yy], gx_r.at[2, yy])
            passed = grecv[2, yy].astype(F32)
            if k in SUM_RIGHT:
                to_r += passed
            else:
                to_l += passed
        gsend[1, yy] = to_r.astype(BF16)
        gsend[2, yy] = to_l.astype(BF16)
        send(gsend.at[1, yy], grecv.at[0, yy], gx_s.at[1, yy], gx_r.at[0, yy], to_right)
        send(gsend.at[2, yy], grecv.at[1, yy], gx_s.at[2, yy], gx_r.at[1, yy], to_left)
    gown[...] = term(x)

    wait(ibuf.at[1], img_r.at[1])
    wait(ibuf.at[5], img_r.at[5])
    img_pass = 2 * c
    send(ibuf.at[1], ibuf.at[img_pass], img_s.at[3], img_r.at[img_pass], sib)
    img_from, img_on = 5 - 4 * c, 4 - 4 * c
    send(ibuf.at[img_from], ibuf.at[img_on], img_s.at[4], img_r.at[img_on], ring(1))

    def sum_x(k, yy):
        total = gown[yy]
        for n in (0, 1, 2) if k in SUM_NONE else (0, 1):
            wait(grecv.at[n, yy], gx_r.at[n, yy])
            total += grecv[n, yy].astype(F32)
        return total

    for k, e in enumerate(eorder[:-1]):
        yy = (y + e) % ny
        ysend[yy] = sum_x(k, yy).astype(BF16)
        send(ysend.at[yy], yrecv.at[y], gy_s.at[yy], gy_r.at[y], device(x, yy, z, c))
    yown[...] = sum_x(ny - 1, y)

    own_grad = grad2[c]
    to_a = dot_t(own_grad[:, :HALF], wbuf[0]) + dot_t(own_grad[:, HALF:], wbuf[1, :, : 2 * LANES])
    to_b = dot_t(own_grad, bpart[...])
    pooled_grad_ref[...] = (dot_t(to_a.astype(BF16), pick_a) + dot_t(to_b.astype(BF16), pick_b)).astype(BF16)

    stores[0].start()

    total = yown[...]
    for e in ydist:
        yy = (y + e) % ny
        wait(yrecv.at[yy], gy_r.at[yy])
        total += yrecv[yy].astype(F32)
    zsend[...] = jnp.zeros_like(zsend)
    for t in range(TILES):
        part = total[:nz] if t < 7 else total[nz:]
        zsend[pl.ds(t, nz, stride=16), :] = part[:, (t % 7) * LANES : (t % 7 + 1) * LANES]

    def zrow(zz):
        return zsend.at[pl.ds(pl.multiple_of(zz * 16, 16), 16), :]

    for e in ring_order(nz):
        zz = (z + e) % nz
        send(zrow(zz), zrecv.at[z], gz_s.at[zz], gz_r.at[z], device(x, y, zz, c))

    for k in (0, 2, 4):
        wait(ibuf.at[k], img_r.at[k])
    text_emb_grad = pairs(tbuf[2], ibuf[...].reshape(WINDOW * tok, D), 3)
    text_again = text_ref[...].astype(F32)
    again_inv = 1.0 / jnp.sqrt(jnp.sum(text_again * text_again, axis=1, keepdims=True) + EPS)
    text_unit = text_again * again_inv
    text_grad_ref[...] = (
        text_emb_grad - text_unit * jnp.sum(text_unit * text_emb_grad, axis=1, keepdims=True)
    ) * again_inv
    stores[1].start()

    summed = zsend[pl.ds(pl.multiple_of(z * 16, 16), 16), :]
    for e in ring_order(nz):
        zz = (z + e) % nz
        wait(zrecv.at[zz], gz_r.at[zz])
        summed += zrecv[zz]
    turned = pltpu.roll(summed, LANES // 2, 1)
    low = lax.broadcasted_iota(jnp.int32, (1, LANES), 1) < LANES // 2
    for b in range(TILES):
        first, second = (9 + b) % TILES, (10 + b) % TILES
        odd_row = jnp.where(low, turned[first : first + 1], turned[second : second + 1])
        row_b = jnp.where(c == 0, summed[b : b + 1], odd_row)
        width = min(LANES, GROUP - b * LANES)
        weight_grad_ref[:, b * LANES : b * LANES + width] = row_b[:, :width]
    stores[2].start()

    for ref, sem in sent:
        wait(ref, sem)
    for store in stores:
        store.wait()


def finish_kernel(a, b, c, a_out, b_out, c_out, a_held, b_held, c_held, in_sem, out_sem):
    parts = [(a, a_held, a_out), (b, b_held, b_out), (c, c_held, c_out)]
    loads = [pltpu.make_async_copy(src, held, in_sem.at[k]) for k, (src, held, _) in enumerate(parts)]
    stores = [pltpu.make_async_copy(held, dst, out_sem.at[k]) for k, (_, held, dst) in enumerate(parts)]
    for load in loads:
        load.start()
    for load, store in zip(loads, stores):
        load.wait()
        store.start()
    for store in stores:
        store.wait()


def body(dims, pooled, other_part, head_weight, text, logit_scale, logit_bias):
    nx, ny, nz = dims
    count = 2 * nx * ny * nz
    tok, kw = pooled.shape
    rows = 2 * nz
    dma = lambda *shape: pltpu.SemaphoreType.DMA(shape)
    hbm = pl.BlockSpec(memory_space=pltpu.HBM)
    smem = pl.BlockSpec(memory_space=pltpu.SMEM)
    made = pl.pallas_call(
        functools.partial(kernel, dims),
        out_shape=(
            jax.ShapeDtypeStruct((tok, kw), BF16),
            jax.ShapeDtypeStruct((tok, D), F32),
            jax.ShapeDtypeStruct((1, GROUP), F32),
        ),
        in_specs=[hbm, hbm, hbm, hbm, smem, smem],
        out_specs=(hbm, hbm, hbm),
        scratch_shapes=[
            pltpu.VMEM((tok, kw), BF16),
            pltpu.VMEM((tok, D), BF16),
            pltpu.VMEM((1, GROUP), BF16),
            pltpu.VMEM((tok, D), BF16),
            pltpu.VMEM((tok, kw), BF16),
            pltpu.VMEM((tok, D), F32),
            pltpu.VMEM((1, GROUP), F32),
            pltpu.VMEM((16, LANES), F32),
            pltpu.VMEM((rows, 16, LANES), BF16),
            pltpu.VMEM((2, count, HALF), BF16),
            pltpu.VMEM((count // 2, D), BF16),
            pltpu.VMEM((WINDOW, tok, D), BF16),
            pltpu.VMEM((WINDOW, tok, D), BF16),
            pltpu.VMEM((2, tok, kw), BF16),
            pltpu.VMEM((2, tok, D), BF16),
            pltpu.VMEM((tok, kw), BF16),
            pltpu.VMEM((count // 2, 2 * tok), BF16),
            pltpu.VMEM((count // 2, 2 * tok), BF16),
            pltpu.VMEM((3, ny, rows, HALF), BF16),
            pltpu.VMEM((2, ny, rows, HALF), F32),
            pltpu.VMEM((ny, rows, HALF), F32),
            pltpu.VMEM((3, ny, rows, HALF), BF16),
            pltpu.VMEM((ny, rows, HALF), BF16),
            pltpu.VMEM((rows, HALF), F32),
            pltpu.VMEM((ny, rows, HALF), BF16),
            pltpu.VMEM((nz * 16, LANES), F32),
            pltpu.VMEM((nz, 16, LANES), F32),
            dma(rows), dma(rows),
            dma(ny), dma(ny),
            dma(ny, 3), dma(nx, ny),
            dma(3 + ny), dma(nx),
            dma(5), dma(WINDOW),
            dma(5), dma(WINDOW),
            dma(2), dma(2),
            dma(3, ny), dma(3, ny),
            dma(ny), dma(ny),
            dma(nz), dma(nz),
            dma(4),
            dma(3),
            dma(4), dma(4),
        ],
        compiler_params=pltpu.CompilerParams(
            collective_id=0, has_side_effects=True, vmem_limit_bytes=60 * 1024 * 1024
        ),
    )(pooled, other_part, head_weight, text, logit_scale, logit_bias)
    return pl.pallas_call(
        finish_kernel,
        out_shape=tuple(jax.ShapeDtypeStruct(m.shape, m.dtype) for m in made),
        in_specs=[hbm, hbm, hbm],
        out_specs=(hbm, hbm, hbm),
        scratch_shapes=[pltpu.VMEM(m.shape, m.dtype) for m in made] + [dma(3), dma(3)],
        compiler_params=pltpu.CompilerParams(vmem_limit_bytes=60 * 1024 * 1024),
    )(*made)


def solution(mesh, dims=(X, Y, Z)):
    return jax.shard_map(
        functools.partial(body, dims),
        mesh=mesh,
        in_specs=(P("dp", None), P("dp", None), P("dp", None), P("dp", None), P(), P()),
        out_specs=(P("dp", None), P("dp", None), P("dp", None)),
        check_vma=False,
    )
```
